32 devices in a mesh: replica: 2 (over core), shard: 16 (over z, y, x).
Axes of the slice: x: 2, y: 2, z: 4, core: 2. Of those that a mesh axis runs over, the one named last changes fastest.
Arguments:
- features: bfloat16 [64, 544, 512], P(('replica', 'shard')), may hold values from -20 to 20
- frame_times: int32 [64, 544], P(('replica', 'shard')), may hold values from 0 to 1692, as said below
- cotangent: bfloat16 [64, 544, 512], P(('replica', 'shard')), may hold values from -20 to 20
- vectors: bfloat16 [9, 512], P(None, 'shard'), may hold values from 0.25 to 1.75
- first_up: bfloat16 [512, 2048], P('shard'), may hold values from -0.25 to 0.25
- first_down: bfloat16 [2048, 512], P('shard'), may hold values from -0.25 to 0.25
- query_key_value: bfloat16 [512, 1536], P('shard'), may hold values from -0.25 to 0.25
- place_weight: bfloat16 [512, 512], P('shard'), may hold values from -0.25 to 0.25
- out_weight: bfloat16 [512, 512], P('shard'), may hold values from -1 to 1
- point_glu: bfloat16 [512, 1024], P('shard'), may hold values from -0.25 to 0.25
- depth_taps: bfloat16 [31, 512], P(None, 'shard'), may hold values from -1 to 1
- point_out: bfloat16 [512, 512], P('shard'), may hold values from -0.5 to 0.5
- second_up: bfloat16 [512, 2048], P('shard'), may hold values from -0.25 to 0.25
- second_down: bfloat16 [2048, 512], P('shard'), may hold values from -0.25 to 0.25
Outputs:
- output: bfloat16 [64, 544, 512], P(('replica', 'shard'))
- grad_features: bfloat16 [64, 544, 512], P(('replica', 'shard'))
- grad_vectors: float32 [9, 512], P(None, 'shard')
- grad_first_up: float32 [512, 2048], P('shard')
- grad_first_down: float32 [2048, 512], P('shard')
- grad_query_key_value: float32 [512, 1536], P('shard')
- grad_place_weight: float32 [512, 512], P('shard')
- grad_out_weight: float32 [512, 512], P('shard')
- grad_point_glu: float32 [512, 1024], P('shard')
- grad_depth_taps: float32 [31, 512], P(None, 'shard')
- grad_point_out: float32 [512, 512], P('shard')
- grad_second_up: float32 [512, 2048], P('shard')
- grad_second_down: float32 [2048, 512], P('shard')
The draws below stay inside these ranges and needn't reach their ends.
Inputs may be any that keep to these rules, and one draw needn't show every extreme that they name: `frame_times`: within a clip the frame times rise by 1 to 3 from each token to the next.
All inputs are finite; a program needn't handle non-finite values.
Results may differ from the reference program's by a relative error of at most 0.04.
Values may be sent and summed in bfloat16 or wider, within the bound.
A program may use at most 256 MiB of HBM per device.

```python
import math
import jax
import jax.numpy as jnp
from jax import lax

D = 512
HEADS = 8
HEAD_DIM = 64
FF = 2048
KERNEL = 31
NVEC = 9
CLIP_LEN = 544
HALF = 256
CLIPS = 64


def drifting(key, ramp_top):
    noise_key, common_key = jax.random.split(key)
    full_shape = (CLIPS, CLIP_LEN, D)
    noise = jax.random.normal(noise_key, full_shape, jnp.float32)
    common = jax.random.normal(common_key, (D,), jnp.float32)
    top_level = ramp_top
    ramp = jnp.arange(CLIPS, dtype=jnp.float32) * (top_level / max(CLIPS - 1, 1))
    return noise + ramp[:, None, None] * common[None, None, :]


def draw_features(key, part):
    return drifting(jax.random.fold_in(key, 11), 2.0).astype(jnp.bfloat16)


def draw_cotangent(key, part):
    return drifting(jax.random.fold_in(key, 23), 2.0).astype(jnp.bfloat16)


def draw_frame_times(key, part):
    start_key, step_key = jax.random.split(jax.random.fold_in(key, 37))
    starts = jax.random.randint(start_key, (CLIPS, 1), 0, 64, dtype=jnp.int32)
    starts = starts.at[0, 0].set(0).at[CLIPS - 1, 0].set(63)
    steps_taken = jax.random.randint(step_key, (CLIPS, CLIP_LEN), 1, 4, dtype=jnp.int32)
    steps_taken = steps_taken.at[CLIPS - 1].set(3)
    return (starts + jnp.cumsum(steps_taken, axis=1) - steps_taken[:, :1]).astype(jnp.int32)


def steps_of(stream_key, dims, shards, low, largest):
    gain = 1.0
    for axis_at, shards_of in shards:
        draws = jax.random.uniform(jax.random.fold_in(jax.random.fold_in(stream_key, 6), axis_at), (shards_of,), jnp.float32, low / len(shards), largest / len(shards))
        gain = gain * jnp.repeat(jnp.exp(draws), dims[axis_at] // shards_of).reshape((-1,) + (1,) * (len(dims) - 1 - axis_at))
    return gain


def normal_values(key, shape, scale, bound, cuts=(), held_as=jnp.bfloat16):
    array = jax.random.normal(key, shape, jnp.float32) * scale
    if len(cuts) > 0:
        array = steps_of(key, shape, cuts, -0.22, 0.18) * array
    return jnp.clip(array, min=-bound, max=bound).astype(held_as)


def setup_inputs(seed: int = 0) -> dict:
    splits = jax.random.split(jax.random.key(seed), 15)
    return {
        "features": draw_features(jax.random.fold_in(splits[14], 71), 0),
        "frame_times": draw_frame_times(jax.random.fold_in(splits[14], 71), 0),
        "cotangent": draw_cotangent(jax.random.fold_in(splits[14], 71), 0),
        "vectors": jnp.clip(1.0 + 0.15 * jax.random.normal(splits[3], (NVEC, D), jnp.float32), 0.25, 1.75).astype(jnp.bfloat16),
        "first_up": normal_values(splits[4], (D, FF), D ** -0.5, 0.25, ((0, 16),)),
        "first_down": normal_values(splits[5], (FF, D), (FF // 4) ** -0.5, 0.25, ((0, 16),)),
        "query_key_value": normal_values(splits[6], (D, 3 * D), D ** -0.5, 0.25, ((0, 16),)),
        "place_weight": normal_values(splits[7], (D, D), D ** -0.5, 0.25, ((0, 16),)),
        "out_weight": normal_values(splits[8], (D, D), (D // 16) ** -0.5, 1.0, ((0, 16),)),
        "point_glu": normal_values(splits[9], (D, 2 * D), D ** -0.5, 0.25, ((0, 16),)),
        "depth_taps": normal_values(splits[10], (KERNEL, D), KERNEL ** -0.5, 1.0, ((1, 16),)),
        "point_out": normal_values(splits[11], (D, D), (D // 4) ** -0.5, 0.5, ((0, 16),)),
        "second_up": normal_values(splits[12], (D, FF), D ** -0.5, 0.25, ((0, 16),)),
        "second_down": normal_values(splits[13], (FF, D), (FF // 4) ** -0.5, 0.25, ((0, 16),)),
    }


epsilon = 1e-05
highest = lax.Precision.HIGHEST

@jax.custom_vjp
def low(v):
    return lax.optimization_barrier(v.astype(jnp.bfloat16)).astype(jnp.float32)

@jax.custom_vjp
def low_back(v):
    return v

def low_keep(v):
    return (low(v), None)

def low_pass(kept, grad):
    return (grad,)

def back_keep(v):
    return (v, None)

def back_low(kept, grad):
    return (low(grad),)
low.defvjp(low_keep, low_pass)
low_back.defvjp(back_keep, back_low)

def normalize(values, gain_row):
    center = values - lax.optimization_barrier(jnp.mean(values, axis=-1, keepdims=True))
    spread = lax.optimization_barrier(jnp.mean(center * center, axis=-1, keepdims=True))
    return center * lax.rsqrt(spread + epsilon) * gain_row

def swish_act(values):
    return values * jax.nn.sigmoid(values)

def wave_table(frame_pos):
    half_width = D // 2
    frequency = jnp.exp(jnp.arange(half_width, dtype=jnp.float32) * (-math.log(10000.0) / half_width))
    angles = frame_pos.astype(jnp.float32)[:, None] * frequency[None, :]
    return (jnp.sin(angles), jnp.cos(angles))

def depthwise(gated_rows, tap_weights):
    tap_count = tap_weights.shape[0]
    reach_left = tap_count // 2
    clip_length = gated_rows.shape[1]
    padded = jnp.pad(gated_rows, ((0, 0), (reach_left, tap_count - 1 - reach_left), (0, 0)))
    running_sum = jnp.zeros_like(gated_rows)
    for offset in range(tap_count):
        running_sum = running_sum + tap_weights[offset] * padded[:, offset:offset + clip_length]
    return running_sum

def gated_conv(mixed_rows, tap_weights):
    half_width = mixed_rows.shape[-1] // 2
    gated_rows = mixed_rows[..., :half_width] * jax.nn.sigmoid(mixed_rows[..., half_width:])
    return depthwise(gated_rows, tap_weights)

def project(values, weight):
    return low_back(jnp.dot(low(values), weight, precision=highest))

def feed_forward(values, gain_row, up_weight, down_weight):
    return project(swish_act(project(normalize(values, gain_row), up_weight)), down_weight)

def attend_clip(joint_rows, frame_pos, u_bias, v_bias, place3):
    clip_length = joint_rows.shape[0]
    head_shape = (clip_length, HEADS, HEAD_DIM)
    query = joint_rows[:, :D]
    query_u = low((query + u_bias).reshape(head_shape))
    query_v = low((query + v_bias).reshape(head_shape))
    key_low = low(joint_rows[:, D:2 * D].reshape(head_shape))
    value_low = low(joint_rows[:, 2 * D:].reshape(head_shape))
    sine_rows, cosines = wave_table(frame_pos)
    raw_place = low_back(jnp.einsum('ihd,ehd->hie', query_v, place3, precision=highest))
    part_sin = raw_place[..., :HALF]
    part_cos = raw_place[..., HALF:]
    coeff = low(jnp.concatenate([part_sin * sine_rows + part_cos * cosines, part_cos * sine_rows - part_sin * cosines], axis=-1))
    basis = low(jnp.concatenate([cosines, sine_rows], axis=-1))
    content = jnp.einsum('ihd,jhd->hij', query_u, key_low, precision=highest)
    placed = jnp.einsum('hie,je->hij', coeff, basis, precision=highest)
    scores = low_back((content + placed) * (1.0 / math.sqrt(HEAD_DIM)))
    prob_values = low(jax.nn.softmax(scores, axis=-1))
    context = low_back(jnp.einsum('hij,jhd->ihd', prob_values, value_low, precision=highest))
    return context.reshape(clip_length, D)

def reference(features, frame_times, cotangent, vectors, first_up, first_down, query_key_value, place_weight, out_weight, point_glu, depth_taps, point_out, second_up, second_down):

    def forward(inputs, gain_rows, up_one, down_one, joint_weight, place_full, out_full, glu_full, tap_weights, point_full, up_two, down_two):
        after_first = inputs + 0.5 * feed_forward(inputs, gain_rows[0], up_one, down_one)
        joint_rows = project(normalize(after_first, gain_rows[1]), joint_weight)
        place3 = place_full.reshape(D, HEADS, HEAD_DIM)

        def one_clip(clip_item):
            return attend_clip(clip_item[0], clip_item[1], gain_rows[2], gain_rows[3], place3)
        context = lax.map(jax.checkpoint(one_clip), (joint_rows, frame_times))
        after_attend = after_first + project(context, out_full)
        mixed_rows = project(normalize(after_attend, gain_rows[4]), glu_full)
        conv_rows = gated_conv(mixed_rows, tap_weights)
        channel_mean = lax.optimization_barrier(jnp.mean(conv_rows, axis=(0, 1)))
        centered = conv_rows - channel_mean
        variance = lax.optimization_barrier(jnp.mean(centered * centered, axis=(0, 1)))
        shaped = centered * lax.rsqrt(variance + epsilon) * gain_rows[5] + gain_rows[6]
        after_conv = after_attend + project(swish_act(shaped), point_full)
        after_second = after_conv + 0.5 * feed_forward(after_conv, gain_rows[7], up_two, down_two)
        return normalize(after_second, gain_rows[8])
    output, pull = jax.vjp(forward, features.astype(jnp.float32), vectors.astype(jnp.float32), first_up.astype(jnp.float32), first_down.astype(jnp.float32), query_key_value.astype(jnp.float32), place_weight.astype(jnp.float32), out_weight.astype(jnp.float32), point_glu.astype(jnp.float32), depth_taps.astype(jnp.float32), point_out.astype(jnp.float32), second_up.astype(jnp.float32), second_down.astype(jnp.float32))
    grads = pull(cotangent.astype(jnp.float32))
    return (output.astype(jnp.bfloat16), grads[0].astype(jnp.bfloat16), grads[1], grads[2], grads[3], grads[4], grads[5], grads[6], grads[7], grads[8], grads[9], grads[10], grads[11])
```

```python
import math

import jax
import jax.numpy as jnp
from jax import lax
from jax.sharding import PartitionSpec as P

HEADS = 8
HEAD_DIM = 64


epsilon = 1e-05


def normalize(values, gain_row):
    center = values - jnp.mean(values, axis=-1, keepdims=True)
    spread = jnp.mean(center * center, axis=-1, keepdims=True)
    return center * lax.rsqrt(spread + epsilon) * gain_row


def normalize_back(values, gain_row, grad_normed):
    pull = jax.vjp(normalize, values, gain_row)[1]
    return pull(grad_normed)


def swish_act(values):
    return values * jax.nn.sigmoid(values)


def swish_slope(values):
    sigmoid = jax.nn.sigmoid(values)
    return sigmoid * (1.0 + values * (1.0 - sigmoid))


def wave_table(frame_pos, model_width):
    half_width = model_width // 2
    frequency = jnp.exp(
        jnp.arange(half_width, dtype=jnp.float32) * (-math.log(10000.0) / half_width)
    )
    angles = frame_pos.astype(jnp.float32)[:, None] * frequency[None, :]
    return (jnp.sin(angles), jnp.cos(angles))


def depthwise(gated_rows, tap_weights):
    tap_count = tap_weights.shape[0]
    reach_left = tap_count // 2
    clip_length = gated_rows.shape[1]
    padded = jnp.pad(gated_rows, ((0, 0), (reach_left, tap_count - 1 - reach_left), (0, 0)))
    running_sum = jnp.zeros_like(gated_rows)
    for offset in range(tap_count):
        running_sum = running_sum + tap_weights[offset] * padded[:, offset : offset + clip_length]
    return running_sum


def gated_conv(mixed_rows, tap_weights):
    half_width = mixed_rows.shape[-1] // 2
    gated_rows = mixed_rows[..., :half_width] * jax.nn.sigmoid(mixed_rows[..., half_width:])
    return depthwise(gated_rows, tap_weights)


def product(left_side, right_side):
    return jnp.dot(left_side, right_side, preferred_element_type=jnp.float32)


def product_left(left_side, right_side):
    return lax.dot_general(
        left_side, right_side, (((0,), (0,)), ((), ())), preferred_element_type=jnp.float32
    )


def product_right(left_side, right_side):
    return lax.dot_general(
        left_side, right_side, (((1,), (1,)), ((), ())), preferred_element_type=jnp.float32
    )


def feed_forward(inputs, gain_row, up_full, down_full):
    normed_low = normalize(inputs, gain_row).astype(jnp.bfloat16)
    hidden = product(normed_low, up_full)
    active_low = swish_act(hidden).astype(jnp.bfloat16)
    return (product(active_low, down_full), (normed_low, hidden, active_low))


def feed_back(grad_stream, inputs, gain_row, up_full, down_full, kept_values):
    normed_low, hidden, active_low = kept_values
    grad_low = (0.5 * grad_stream).astype(jnp.bfloat16)
    grad_down = product_left(active_low, grad_low)
    grad_hidden = (product_right(grad_low, down_full) * swish_slope(hidden)).astype(jnp.bfloat16)
    grad_up = product_left(normed_low, grad_hidden)
    grad_normed = product_right(grad_hidden, up_full)
    grad_extra, grad_gain = normalize_back(inputs, gain_row, grad_normed)
    return (grad_stream + grad_extra, grad_gain, grad_up, grad_down)


def clip_inputs(joint_rows, u_bias, v_bias):
    clip_length = joint_rows.shape[0]
    model_width = joint_rows.shape[1] // 3
    head_shape = (clip_length, HEADS, model_width // HEADS)
    query = joint_rows[:, :model_width]
    query_u = (query + u_bias).reshape(head_shape).astype(jnp.bfloat16)
    query_v = (query + v_bias).reshape(head_shape).astype(jnp.bfloat16)
    key_low = joint_rows[:, model_width : 2 * model_width].reshape(head_shape).astype(jnp.bfloat16)
    value_low = joint_rows[:, 2 * model_width :].reshape(head_shape).astype(jnp.bfloat16)
    return (query_u, query_v, key_low, value_low)


def clip_scores(query_u, query_v, key_low, place3, frame_pos):
    sine_rows, cosines = wave_table(frame_pos, place3.shape[0])
    raw_place = jnp.einsum("ihd,ehd->hie", query_v, place3, preferred_element_type=jnp.float32)
    half_width = raw_place.shape[-1] // 2
    part_sin = raw_place[..., :half_width]
    part_cos = raw_place[..., half_width:]
    coeff_low = jnp.concatenate(
        [part_sin * sine_rows + part_cos * cosines, part_cos * sine_rows - part_sin * cosines],
        axis=-1,
    ).astype(jnp.bfloat16)
    basis_low = jnp.concatenate([cosines, sine_rows], axis=-1).astype(jnp.bfloat16)
    content = jnp.einsum("ihd,jhd->hij", query_u, key_low, preferred_element_type=jnp.float32)
    placed = jnp.einsum("hie,je->hij", coeff_low, basis_low, preferred_element_type=jnp.float32)
    scores = (content + placed) * (1.0 / math.sqrt(HEAD_DIM))
    return (scores, sine_rows, cosines, basis_low)


def clip_forward(joint_rows, frame_pos, u_bias, v_bias, place3):
    query_u, query_v, key_low, value_low = clip_inputs(joint_rows, u_bias, v_bias)
    scores = clip_scores(query_u, query_v, key_low, place3, frame_pos)[0]
    row_peak = jnp.max(scores, axis=-1, keepdims=True)
    logsum = row_peak + jnp.log(jnp.sum(jnp.exp(scores - row_peak), axis=-1, keepdims=True))
    probs_low = jnp.exp(scores - logsum).astype(jnp.bfloat16)
    context = jnp.einsum("hij,jhd->ihd", probs_low, value_low, preferred_element_type=jnp.float32)
    return (context.reshape(joint_rows.shape[0], -1).astype(jnp.bfloat16), logsum)


def clip_backward(joint_rows, frame_pos, logsum, grad_context, u_bias, v_bias, place3):
    clip_length = joint_rows.shape[0]
    query_u, query_v, key_low, value_low = clip_inputs(joint_rows, u_bias, v_bias)
    scores, sine_rows, cosines, basis_low = clip_scores(
        query_u, query_v, key_low, place3, frame_pos
    )
    prob_values = jnp.exp(scores - logsum)
    probs_low = prob_values.astype(jnp.bfloat16)
    grad_heads = grad_context.reshape(query_u.shape)
    grad_value = jnp.einsum(
        "hij,ihd->jhd", probs_low, grad_heads, preferred_element_type=jnp.float32
    )
    grad_probs = jnp.einsum(
        "ihd,jhd->hij", grad_heads, value_low, preferred_element_type=jnp.float32
    )
    inner_sum = jnp.sum(grad_probs * prob_values, axis=-1, keepdims=True)
    grad_scores = (prob_values * (grad_probs - inner_sum)).astype(jnp.bfloat16) * (
        1.0 / math.sqrt(HEAD_DIM)
    )
    grad_query_u = jnp.einsum(
        "hij,jhd->ihd", grad_scores, key_low, preferred_element_type=jnp.float32
    )
    grad_key = jnp.einsum("hij,ihd->jhd", grad_scores, query_u, preferred_element_type=jnp.float32)
    grad_coeff = jnp.einsum(
        "hij,je->hie", grad_scores, basis_low, preferred_element_type=jnp.float32
    )
    half_width = grad_coeff.shape[-1] // 2
    grad_cos_part = grad_coeff[..., :half_width]
    grad_sin_part = grad_coeff[..., half_width:]
    grad_raw = jnp.concatenate(
        [
            grad_cos_part * sine_rows - grad_sin_part * cosines,
            grad_cos_part * cosines + grad_sin_part * sine_rows,
        ],
        axis=-1,
    ).astype(jnp.bfloat16)
    grad_query_v = jnp.einsum("hie,ehd->ihd", grad_raw, place3, preferred_element_type=jnp.float32)
    grad_place = jnp.einsum("hie,ihd->ehd", grad_raw, query_v, preferred_element_type=jnp.float32)
    grad_joint = jnp.concatenate(
        [
            (grad_query_u + grad_query_v).reshape(clip_length, -1),
            grad_key.reshape(clip_length, -1),
            grad_value.reshape(clip_length, -1),
        ],
        axis=-1,
    )
    return (
        grad_joint,
        jnp.sum(grad_query_u, axis=0).reshape(-1),
        jnp.sum(grad_query_v, axis=0).reshape(-1),
        grad_place,
    )


def fold_down(rows, parts, depth):
    blocks = rows.reshape(parts, -1, depth, rows.shape[-1])
    return blocks.transpose(0, 2, 1, 3).reshape(parts * depth, -1)


def unfold_down(block, parts, width):
    depth = block.shape[0] // parts
    pieces = block.reshape(parts, depth, -1, width)
    return pieces.transpose(0, 2, 1, 3).reshape(-1, width)


def pack_small(columns):
    joined = jnp.concatenate(columns, axis=1)
    return jnp.pad(joined, ((0, 0), (0, -joined.shape[1] % 128)))


def split_columns(block, widths):
    pieces = []
    start = 0
    for width in widths:
        pieces.append(block[:, start : start + width])
        start += width
    return pieces


def body(
    features,
    frame_times,
    cotangent,
    vectors,
    first_up,
    first_down,
    query_key_value,
    place_weight,
    out_weight,
    point_glu,
    depth_taps,
    point_out,
    second_up,
    second_down,
):
    clip_count, clip_length, model_width = features.shape
    row_count = clip_count * clip_length
    token_count = row_count * lax.axis_size("replica") * lax.axis_size("shard")

    shards = lax.axis_size("shard")
    depth = first_up.shape[0]
    hidden_width = first_up.shape[1]
    row_total = vectors.shape[0]
    tap_total = depth_taps.shape[0]

    early = jnp.concatenate(
        [
            first_up,
            fold_down(first_down, 1, depth),
            query_key_value,
            place_weight,
            out_weight,
            pack_small([vectors.T, depth_taps.T]),
        ],
        axis=1,
    )
    late = jnp.concatenate(
        [point_glu, point_out, second_up, fold_down(second_down, 1, depth)], axis=1
    )
    early_full = lax.all_gather(early, "shard", axis=0, tiled=True)
    late_full = lax.all_gather(late, "shard", axis=0, tiled=True)
    pieces = split_columns(
        early_full,
        (hidden_width, hidden_width, 3 * model_width, model_width, model_width, 128),
    )
    small = pieces[5].T
    first_full = (
        small[:row_total],
        pieces[0],
        unfold_down(pieces[1], shards, model_width),
    )
    attend_full = (pieces[2], pieces[3], pieces[4])
    pieces = split_columns(late_full, (2 * model_width, model_width, hidden_width, hidden_width))
    conv_full = (pieces[0], small[row_total : row_total + tap_total], pieces[1])
    second_full = (pieces[2], unfold_down(pieces[3], shards, model_width))
    gains = first_full[0].astype(jnp.float32)
    inputs = features.reshape(row_count, model_width).astype(jnp.float32)
    first_out, first_kept = feed_forward(inputs, gains[0], first_full[1], first_full[2])
    after_first = inputs + 0.5 * first_out
    normed_attend = normalize(after_first, gains[1]).astype(jnp.bfloat16)
    joint_rows = product(normed_attend, attend_full[0])
    joint_clips = joint_rows.reshape(clip_count, clip_length, 3 * model_width)
    place_full = attend_full[1].reshape(model_width, HEADS, model_width // HEADS)

    def forward_clip(clip_item):
        return clip_forward(clip_item[0], clip_item[1], gains[2], gains[3], place_full)

    context_clips, logsum_clips = lax.map(forward_clip, (joint_clips, frame_times))
    context_low = context_clips.reshape(row_count, model_width)
    after_attend = after_first + product(context_low, attend_full[2])
    normed_conv = normalize(after_attend, gains[4]).astype(jnp.bfloat16)
    mixed_rows = product(normed_conv, conv_full[0]).reshape(
        clip_count, clip_length, 2 * model_width
    )
    conv_flat = gated_conv(mixed_rows, conv_full[1].astype(jnp.float32)).reshape(
        row_count, model_width
    )
    channel_mean = lax.psum(jnp.sum(conv_flat, axis=0), ("replica", "shard")) / token_count
    centered = conv_flat - channel_mean
    variance = lax.psum(jnp.sum(centered * centered, axis=0), ("replica", "shard")) / token_count
    inverse = lax.rsqrt(variance + epsilon)
    unit_values = centered * inverse
    shaped = unit_values * gains[5] + gains[6]
    active_conv = swish_act(shaped).astype(jnp.bfloat16)
    after_conv = after_attend + product(active_conv, conv_full[2])
    second_out, second_kept = feed_forward(after_conv, gains[7], second_full[0], second_full[1])
    after_second = after_conv + 0.5 * second_out
    output = normalize(after_second, gains[8])
    grad_last, grad_final_gain = normalize_back(
        after_second, gains[8], cotangent.reshape(row_count, model_width).astype(jnp.float32)
    )
    second_back = second_full
    grad_conv_out, grad_second_gain, grad_second_up, grad_second_down = feed_back(
        grad_last, after_conv, gains[7], second_back[0], second_back[1], second_kept
    )
    conv_back = conv_full
    grad_low = grad_conv_out.astype(jnp.bfloat16)
    grad_point_out = product_left(active_conv, grad_low)
    grad_shaped = product_right(grad_low, conv_back[2]) * swish_slope(shaped)
    shift_total, gain_total = lax.psum(
        (jnp.sum(grad_shaped, axis=0), jnp.sum(grad_shaped * unit_values, axis=0)),
        ("replica", "shard"),
    )
    grad_conv = (
        gains[5]
        * inverse
        * (grad_shaped - shift_total / token_count - unit_values * (gain_total / token_count))
    )
    pull_conv = jax.vjp(gated_conv, mixed_rows, conv_back[1].astype(jnp.float32))[1]
    grad_mixed, grad_taps = pull_conv(grad_conv.reshape(clip_count, clip_length, model_width))
    grad_mixed_low = grad_mixed.reshape(row_count, 2 * model_width).astype(jnp.bfloat16)
    grad_point_glu = product_left(normed_conv, grad_mixed_low)
    grad_extra, grad_conv_gain = normalize_back(
        after_attend, gains[4], product_right(grad_mixed_low, conv_back[0])
    )
    grad_attend_out = grad_conv_out + grad_extra
    late_grads = jnp.concatenate(
        [
            grad_point_glu.astype(jnp.bfloat16),
            grad_point_out.astype(jnp.bfloat16),
            grad_second_up.astype(jnp.bfloat16),
            fold_down(grad_second_down.astype(jnp.bfloat16), shards, depth),
            pack_small([grad_taps.T.astype(jnp.bfloat16)]),
        ],
        axis=1,
    )
    late_grads, grad_attend_out = lax.optimization_barrier((late_grads, grad_attend_out))
    late_sums = lax.psum_scatter(late_grads, "shard", scatter_dimension=0, tiled=True)
    attend_back = attend_full
    grad_low = grad_attend_out.astype(jnp.bfloat16)
    grad_out_weight = product_left(context_low, grad_low)
    grad_context = (
        product_right(grad_low, attend_back[2])
        .astype(jnp.bfloat16)
        .reshape(clip_count, clip_length, model_width)
    )
    place_back = attend_back[1].reshape(model_width, HEADS, model_width // HEADS)

    def backward_clip(running, clip_item):
        grad_joint, grad_u, grad_v, grad_place = clip_backward(
            clip_item[0], clip_item[1], clip_item[2], clip_item[3], gains[2], gains[3], place_back
        )
        return ((running[0] + grad_u, running[1] + grad_v, running[2] + grad_place), grad_joint)

    start_sums = (
        jnp.zeros((model_width,), jnp.float32),
        jnp.zeros((model_width,), jnp.float32),
        jnp.zeros(place_back.shape, jnp.float32),
    )
    bias_sums, grad_joint_clips = lax.scan(
        backward_clip, start_sums, (joint_clips, frame_times, logsum_clips, grad_context)
    )
    grad_joint_low = grad_joint_clips.reshape(row_count, 3 * model_width).astype(jnp.bfloat16)
    grad_qkv = product_left(normed_attend, grad_joint_low)
    grad_extra, grad_attend_gain = normalize_back(
        after_first, gains[1], product_right(grad_joint_low, attend_back[0])
    )
    grad_first_out = grad_attend_out + grad_extra
    grad_place_full = bias_sums[2].reshape(model_width, model_width)
    first_back = first_full
    first_gains = first_back[0].astype(jnp.float32)
    grad_inputs, grad_first_gain, grad_first_up, grad_first_down = feed_back(
        grad_first_out, inputs, first_gains[0], first_back[1], first_back[2], first_kept
    )
    zero_row = jnp.zeros_like(grad_first_gain)
    grad_rows = jnp.stack(
        [
            grad_first_gain,
            grad_attend_gain,
            bias_sums[0],
            bias_sums[1],
            grad_conv_gain,
            zero_row,
            zero_row,
            grad_second_gain,
            grad_final_gain,
        ]
    )
    early_grads = jnp.concatenate(
        [
            grad_first_up.astype(jnp.bfloat16),
            fold_down(grad_first_down.astype(jnp.bfloat16), shards, depth),
            grad_qkv.astype(jnp.bfloat16),
            grad_place_full.astype(jnp.bfloat16),
            grad_out_weight.astype(jnp.bfloat16),
            pack_small([grad_rows.T.astype(jnp.bfloat16)]),
        ],
        axis=1,
    )
    early_sums = lax.psum_scatter(early_grads, "shard", scatter_dimension=0, tiled=True)
    late_total = lax.psum(late_sums, "replica").astype(jnp.float32)
    early_total = lax.psum(early_sums, "replica").astype(jnp.float32)
    pieces = split_columns(
        early_total,
        (hidden_width, hidden_width, 3 * model_width, model_width, model_width, row_total),
    )
    late_pieces = split_columns(
        late_total, (2 * model_width, model_width, hidden_width, hidden_width, tap_total)
    )
    summed = (
        pieces[5].T,
        pieces[0],
        unfold_down(pieces[1], 1, model_width),
        pieces[2],
        pieces[3],
        pieces[4],
        late_pieces[0],
        late_pieces[4].T,
        late_pieces[1],
        late_pieces[2],
        unfold_down(late_pieces[3], 1, model_width),
    )
    shard_cols = summed[0].shape[1]
    first_col = lax.axis_index("shard") * shard_cols
    gain_part = lax.dynamic_slice_in_dim(gain_total, first_col, shard_cols)
    shift_part = lax.dynamic_slice_in_dim(shift_total, first_col, shard_cols)
    grad_vectors = summed[0].at[5].add(gain_part).at[6].add(shift_part)
    return (
        output.astype(jnp.bfloat16).reshape(clip_count, clip_length, model_width),
        grad_inputs.astype(jnp.bfloat16).reshape(clip_count, clip_length, model_width),
        grad_vectors,
        summed[1],
        summed[2],
        summed[3],
        summed[4],
        summed[5],
        summed[6],
        summed[7],
        summed[8],
        summed[9],
        summed[10],
    )


def solution(mesh):
    return jax.shard_map(
        body,
        mesh=mesh,
        in_specs=(
            P(("replica", "shard"), None, None),
            P(("replica", "shard"), None),
            P(("replica", "shard"), None, None),
            P(None, "shard"),
            P("shard", None),
            P("shard", None),
            P("shard", None),
            P("shard", None),
            P("shard", None),
            P("shard", None),
            P(None, "shard"),
            P("shard", None),
            P("shard", None),
            P("shard", None),
        ),
        out_specs=(
            P(("replica", "shard"), None, None),
            P(("replica", "shard"), None, None),
            P(None, "shard"),
            P("shard", None),
            P("shard", None),
            P("shard", None),
            P("shard", None),
            P("shard", None),
            P("shard", None),
            P(None, "shard"),
            P("shard", None),
            P("shard", None),
            P("shard", None),
        ),
        check_vma=False,
    )
```
